32 devices in a mesh: dp: 8 (over z, y), seq: 4 (over x, core).
Axes of the slice: x: 2, y: 2, z: 4, core: 2. Of those that a mesh axis runs over, the one named last changes fastest.
Arguments:
- queries: bfloat16 [8, 1024, 4096], P('dp', 'seq'), may hold values from -12 to 12
- key_states: bfloat16 [8, 1024, 512], P('dp', 'seq'), may hold values from -12 to 12
- value_states: bfloat16 [8, 1024, 512], P('dp', 'seq'), may hold values from -6 to 6
- out_grad: bfloat16 [8, 1024, 4096], P('dp', 'seq'), may hold values from -6 to 6
- layer_input: bfloat16 [8, 1024, 8192], P('dp', 'seq'), may hold values from -6 to 6
- lengths: int32 [8, 8], P('dp'), may hold values from 1 to 512, 1024 in all within a row
Outputs:
- query_grad: bfloat16 [8, 1024, 4096], P('dp', 'seq')
- key_grad: bfloat16 [8, 1024, 512], P('dp', 'seq')
- value_grad: bfloat16 [8, 1024, 512], P('dp', 'seq')
- value_weight_grad: float32 [8192, 512], P(('dp', 'seq'))
The draws below stay inside these ranges and needn't reach their ends.
Inputs may be any that keep to these rules, and one draw needn't show every extreme that they name: `lengths`: each row sums to 1024 and its largest entry is exactly 512.
All inputs are finite; a program needn't handle non-finite values.
Results may differ from the reference program's by a relative error of at most 0.018.
Values may be sent and summed in bfloat16 or wider, within the bound.
A program may use at most 192 MiB of HBM per device.

```python
import math
import jax
import jax.numpy as jnp
import numpy as np
from jax import lax

D = 8192
HQ = 32
HK = 4
HD = 128
LEN = 1024
SAMPLES = 8
STREAMS = 8
MOST = 512


def draw_queries(key, part):
    gaussian = jax.random.normal(jax.random.fold_in(key, 11), (STREAMS, LEN, HQ, HD), jnp.float32)
    return jnp.clip(gaussian, -12.0, 12.0).reshape(STREAMS, LEN, HQ * HD).astype(jnp.bfloat16)


def draw_key_states(key, part):
    gaussian = jax.random.normal(jax.random.fold_in(key, 13), (STREAMS, LEN, HK, HD), jnp.float32)
    return jnp.clip(gaussian, -12.0, 12.0).reshape(STREAMS, LEN, HK * HD).astype(jnp.bfloat16)


def shard_levels(own_key, dims, cuts, smallest, largest):
    factor_of, own = 1.0, jax.random.fold_in(own_key, 6)
    for axis_at, blocks in cuts:
        steps = jnp.exp(jax.random.uniform(jax.random.fold_in(own, axis_at), (blocks,), jnp.float32, smallest / len(cuts), largest / len(cuts)))
        factor_of = factor_of * jnp.repeat(steps, dims[axis_at] // blocks).reshape([-1 if axis == axis_at else 1 for axis in range(len(dims))])
    return factor_of


def profile(number_of, total, most, slope):
    loads = [(1 << 20) // math.isqrt(standing ** slope) + 1 for standing in range(2, number_of + 1)]
    spare, given = total - most - (number_of - 1), [1] * (number_of - 1)
    while spare > 0:
        candidates = [i for i in range(number_of - 1) if given[i] < most]
        mass, budget = sum([loads[i] for i in candidates]), spare
        for i in candidates:
            addition = min(most - given[i], max(1, budget * loads[i] // mass), spare)
            given[i] = given[i] + addition
            spare = spare - addition
    return np.array([most] + given)


def ragged(own_key, count, total, limit, lean):
    if count == 2:
        one = jax.random.randint(own_key, (), max(1, total - limit), min(limit, total - 1) + 1)
        return jnp.stack([one, total - one])
    sizes = jnp.asarray(profile(count, total, limit, lean), jnp.int32)
    pairs = (count - 1) // 2
    donor, sink = sizes[1:1 + 2 * pairs:2], sizes[2:2 + 2 * pairs:2]
    slack = jnp.minimum(donor - 1, limit - sink)
    moved = jax.random.randint(jax.random.fold_in(own_key, 1), (pairs,), 0, 1 << 20) % (slack + 1)
    sizes = sizes.at[1:1 + 2 * pairs:2].set(donor - moved).at[2:2 + 2 * pairs:2].set(sink + moved)
    return sizes[jax.random.permutation(jax.random.fold_in(own_key, 2), count)]


def normal_values(stream_key, dims, width, limit, cuts=(), kind=jnp.bfloat16):
    values = jax.random.normal(stream_key, dims, jnp.float32) * width
    if len(cuts) > 0:
        values = shard_levels(stream_key, dims, cuts, -0.22, 0.18) * values
    return jnp.clip(values, min=-limit, max=limit).astype(kind)


def setup_inputs(seed: int = 0) -> dict:
    splits = jax.random.split(jax.random.key(seed), 7)
    queries = draw_queries(jax.random.fold_in(splits[6], 71), 0)
    key_states = draw_key_states(jax.random.fold_in(splits[6], 71), 0)
    value_states = normal_values(splits[2], (STREAMS, LEN, HK * HD), 1.0, 6.0, ((0, 8), (1, 4)))
    out_grad = normal_values(splits[3], (STREAMS, LEN, HQ * HD), 1.0, 6.0, ((0, 8), (1, 4)))
    layer_input = normal_values(splits[4], (STREAMS, LEN, D), 1.0, 6.0, ((0, 8), (1, 4)))
    lengths = jax.vmap(lambda own: ragged(own, SAMPLES, LEN, MOST, 2))(jax.random.split(splits[5], STREAMS)).reshape((STREAMS, SAMPLES)).astype(jnp.int32)
    return {"queries": queries, "key_states": key_states, "value_states": value_states, "out_grad": out_grad, "layer_input": layer_input, "lengths": lengths}


def segment_ids_of(lengths):
    sample_ends = jnp.cumsum(lengths).astype(jnp.int32)
    positions = jnp.arange(LEN, dtype=jnp.int32)
    return lax.optimization_barrier(jnp.sum((sample_ends[None, :] <= positions[:, None]).astype(jnp.int32), axis=1))

def stream_grads(operands):
    queries, key_states, value_states, out_grad, lengths = operands
    group_size = HQ // HK
    score_scale = HD ** (-0.5)
    segment_ids = segment_ids_of(lengths)
    positions = jnp.arange(LEN, dtype=jnp.int32)
    allowed = (segment_ids[:, None] == segment_ids[None, :]) & (positions[None, :] <= positions[:, None])
    query_all = queries.reshape(LEN, HK, group_size, HD)
    grad_all = out_grad.reshape(LEN, HK, group_size, HD)
    key_all = key_states.reshape(LEN, HK, HD)
    value_all = value_states.reshape(LEN, HK, HD)
    query_list, key_list, value_list = ([], [], [])
    for group_index in range(HK):
        query_group = query_all[:, group_index].astype(jnp.float32)
        grad_group = grad_all[:, group_index].astype(jnp.float32)
        key_group = key_all[:, group_index].astype(jnp.float32)
        value_group = value_all[:, group_index].astype(jnp.float32)
        scores = jnp.einsum('qgd,kd->gqk', query_group, key_group) * score_scale
        scores = jnp.where(allowed[None], scores, -jnp.inf)
        row_peak = lax.optimization_barrier(jnp.max(scores, axis=-1, keepdims=True))
        exponent = jnp.exp(scores - row_peak)
        attn_weights = exponent / lax.optimization_barrier(jnp.sum(exponent, axis=-1, keepdims=True))
        prob_grad = jnp.einsum('qgd,kd->gqk', grad_group, value_group)
        row_delta = lax.optimization_barrier(jnp.sum(attn_weights * prob_grad, axis=-1, keepdims=True))
        score_grad = (attn_weights * (prob_grad - row_delta) * score_scale).astype(jnp.bfloat16)
        weights_half = attn_weights.astype(jnp.bfloat16)
        query_list.append(jnp.einsum('gqk,kd->qgd', score_grad.astype(jnp.float32), key_group).astype(jnp.bfloat16))
        key_part = jnp.einsum('gqk,qgd->gkd', score_grad.astype(jnp.float32), query_group).astype(jnp.bfloat16)
        value_part = jnp.einsum('gqk,qgd->gkd', weights_half.astype(jnp.float32), grad_group).astype(jnp.bfloat16)
        key_list.append(lax.optimization_barrier(jnp.sum(key_part.astype(jnp.float32), axis=0)).astype(jnp.bfloat16))
        value_list.append(lax.optimization_barrier(jnp.sum(value_part.astype(jnp.float32), axis=0)).astype(jnp.bfloat16))
    query_grad = jnp.stack(query_list, axis=1).reshape(LEN, HQ * HD)
    key_grad = jnp.stack(key_list, axis=1).reshape(LEN, HK * HD)
    value_grad = jnp.stack(value_list, axis=1).reshape(LEN, HK * HD)
    return (query_grad, key_grad, value_grad)

def reference(queries, key_states, value_states, out_grad, layer_input, lengths):
    query_grad, key_grad, value_grad = lax.map(stream_grads, (queries, key_states, value_states, out_grad, lengths))
    flat_input = layer_input.reshape(STREAMS * LEN, D)
    flat_value = value_grad.reshape(STREAMS * LEN, HK * HD)
    weight_sum = jnp.dot(flat_input.T, flat_value, preferred_element_type=jnp.float32)
    value_weight_grad = weight_sum / math.sqrt(STREAMS * LEN)
    return (query_grad, key_grad, value_grad, value_weight_grad)
```

```python
import functools
import math

import jax
import jax.numpy as jnp
from jax import lax
from jax.experimental import pallas as pl
from jax.experimental.pallas import tpu as pltpu
from jax.sharding import PartitionSpec as P

HD = 128
MOST = 512
SUB = 128
NEG = -1e30


def attention_kernel(
    prior, group, q_ref, g_ref, k_ref, v_ref, sq_ref, sk_ref,
    dq_ref, dkp_ref, dvp_ref, dko_ref, dvo_ref, bias, dk, dv,
):
    local_len = q_ref.shape[0]
    window = k_ref.shape[0]
    span = MOST + SUB
    scale = HD ** (-0.5)
    exp_scale = scale * math.log2(math.e)

    @pl.when(pl.program_id(0) == 0)
    def _():
        key_pos = lax.broadcasted_iota(jnp.int32, (window, local_len), 0) - prior
        row_pos = lax.broadcasted_iota(jnp.int32, (window, local_len), 1)
        allowed = (sk_ref[...] == sq_ref[...]) & (key_pos <= row_pos)
        bias[...] = jnp.where(allowed, 0.0, NEG)

    dk[...] = jnp.zeros_like(dk)
    dv[...] = jnp.zeros_like(dv)
    nt = (((1,), (1,)), ((), ()))
    for r in range(local_len // SUB):
        rows = slice(r * SUB, (r + 1) * SUB)
        start = prior - MOST + r * SUB
        keys = slice(start, start + span)
        k = k_ref[keys, :]
        v = v_ref[keys, :]
        kt = k.T
        part_bias = bias[keys, rows]
        part_bias = jnp.concatenate([part_bias, part_bias], axis=1)
        for pair in range(group // 2):
            a = slice(2 * pair * HD, (2 * pair + 1) * HD)
            b = slice((2 * pair + 1) * HD, (2 * pair + 2) * HD)
            q = jnp.concatenate([q_ref[rows, a], q_ref[rows, b]], axis=0)
            g = jnp.concatenate([g_ref[rows, a], g_ref[rows, b]], axis=0)
            s = lax.dot_general(k, q, nt, preferred_element_type=jnp.float32)
            s = s * exp_scale + part_bias
            e = jnp.exp2(s - jnp.max(s, axis=0, keepdims=True))
            inv = 1.0 / jnp.sum(e, axis=0, keepdims=True)
            dp = lax.dot_general(v, g, nt, preferred_element_type=jnp.float32)
            p = e * inv
            delta = jnp.sum(p * dp, axis=0, keepdims=True)
            ds = (p * ((dp - delta) * scale)).astype(jnp.bfloat16)
            dv[keys, :] += jnp.dot(p.astype(jnp.bfloat16), g, preferred_element_type=jnp.float32)
            dk[keys, :] += jnp.dot(ds, q, preferred_element_type=jnp.float32)
            dqt = jnp.dot(kt, ds, preferred_element_type=jnp.float32)
            dq_ref[rows, a] = dqt[:, :SUB].T.astype(jnp.bfloat16)
            dq_ref[rows, b] = dqt[:, SUB:].T.astype(jnp.bfloat16)
    dkp_ref[...] = dk[:prior, :].astype(jnp.bfloat16)
    dvp_ref[...] = dv[:prior, :].astype(jnp.bfloat16)
    dko_ref[...] = dk[prior:, :]
    dvo_ref[...] = dv[prior:, :]


def attention_grads(q, g, window_kv, seg_rows, seg_keys):
    local_len, width = q.shape
    window = window_kv.shape[0]
    kv_width = window_kv.shape[1] // 2
    kv_heads = kv_width // HD
    group = width // HD // kv_heads
    prior = window - local_len
    wide = lambda n, w: pl.BlockSpec((n, w), lambda i: (0, i))
    whole = lambda s: pl.BlockSpec(s, lambda i: (0, 0))
    elements = window * local_len * kv_heads * group
    return pl.pallas_call(
        functools.partial(attention_kernel, prior, group),
        grid=(kv_heads,),
        in_specs=[
            wide(local_len, group * HD),
            wide(local_len, group * HD),
            wide(window, HD),
            pl.BlockSpec((window, HD), lambda i: (0, i + kv_heads)),
            whole((1, local_len)),
            whole((window, 1)),
        ],
        out_specs=[
            wide(local_len, group * HD),
            wide(prior, HD),
            wide(prior, HD),
            wide(local_len, HD),
            wide(local_len, HD),
        ],
        out_shape=[
            jax.ShapeDtypeStruct((local_len, width), jnp.bfloat16),
            jax.ShapeDtypeStruct((prior, kv_width), jnp.bfloat16),
            jax.ShapeDtypeStruct((prior, kv_width), jnp.bfloat16),
            jax.ShapeDtypeStruct((local_len, kv_width), jnp.float32),
            jax.ShapeDtypeStruct((local_len, kv_width), jnp.float32),
        ],
        scratch_shapes=[
            pltpu.VMEM((window, local_len), jnp.float32),
            pltpu.VMEM((window, HD), jnp.float32),
            pltpu.VMEM((window, HD), jnp.float32),
        ],
        compiler_params=pltpu.CompilerParams(vmem_limit_bytes=40 * 1024 * 1024),
        cost_estimate=pl.CostEstimate(
            flops=10 * elements * HD, bytes_accessed=10 * 1024 * 1024, transcendentals=elements
        ),
    )(q, g, window_kv, window_kv, seg_rows, seg_keys)


def shards(queries, key_states, value_states, out_grad, layer_input, lengths):
    seq_count = lax.axis_size("seq")
    dp_count = lax.axis_size("dp")
    me = lax.axis_index("seq")
    streams, local_len, query_width = queries.shape
    kv_width = key_states.shape[2]
    width = layer_input.shape[2]
    full_len = local_len * seq_count
    steps = -(-MOST // local_len)
    prior = steps * local_len
    piece = width // (dp_count * seq_count)

    own_kv = jnp.concatenate([key_states, value_states], axis=2)
    shifted = [
        lax.ppermute(own_kv, "seq", [(i, i + s) for i in range(seq_count - s)])
        if s < seq_count else jnp.zeros_like(own_kv)
        for s in range(steps, 0, -1)
    ]

    split_input = layer_input.reshape(streams * local_len, dp_count, seq_count, piece)

    def columns_of(owner):
        block = lax.dynamic_slice_in_dim(split_input, owner, 1, axis=2)
        return block.reshape(streams * local_len, dp_count * piece)

    def ring(s):
        return [(i, (i + s) % seq_count) for i in range(seq_count)]

    inputs = [columns_of(me)] + [
        lax.ppermute(columns_of(lax.rem(me + s, seq_count)), "seq", ring(s))
        for s in range(1, seq_count)
    ]
    all_inputs = jnp.concatenate(inputs, axis=0)

    positions = jnp.arange(full_len, dtype=jnp.int32)
    samples = jnp.arange(lengths.shape[1], dtype=jnp.int32)
    ends = jnp.sum(jnp.where(samples[None, :] <= samples[:, None], lengths[:, None, :], 0), axis=2)
    segments = jnp.sum((ends[:, None, :] <= positions[None, :, None]).astype(jnp.int32), axis=2)
    padded = jnp.concatenate([jnp.full((streams, prior), -1, jnp.int32), segments], axis=1)
    seg_window = lax.dynamic_slice_in_dim(padded, me * local_len, prior + local_len, axis=1)

    window_kv = jnp.concatenate(shifted + [own_kv], axis=1)
    results = [
        attention_grads(
            queries[i], out_grad[i], window_kv[i],
            seg_window[i, prior:].reshape(1, local_len), seg_window[i].reshape(-1, 1),
        )
        for i in range(streams)
    ]
    query_grad, key_prior, value_prior, key_own, value_own = (jnp.stack(x) for x in zip(*results))

    def collect(own, parts):
        total = own
        for n, s in enumerate(range(steps, 0, -1)):
            if s < seq_count:
                block = parts[:, n * local_len:(n + 1) * local_len]
                total = total + lax.ppermute(
                    block, "seq", [(i + s, i) for i in range(seq_count - s)]
                ).astype(jnp.float32)
        return total.astype(jnp.bfloat16)

    value_grad = collect(value_own, value_prior)
    key_grad = collect(key_own, key_prior)

    flat_value = value_grad.reshape(streams * local_len, kv_width)
    all_values = jnp.concatenate(
        [flat_value] + [lax.ppermute(flat_value, "seq", ring(s)) for s in range(1, seq_count)],
        axis=0,
    )
    partial = lax.dot_general(
        all_inputs, all_values, (((0,), (0,)), ((), ())), preferred_element_type=jnp.float32
    ) / math.sqrt(streams * dp_count * full_len)
    weight_grad = lax.psum_scatter(
        partial.astype(jnp.bfloat16), "dp", scatter_dimension=0, tiled=True
    ).astype(jnp.float32)
    return (query_grad, key_grad, value_grad, weight_grad)


def solution(mesh):
    token = P("dp", "seq", None)
    return jax.shard_map(
        shards,
        mesh=mesh,
        in_specs=(token, token, token, token, token, P("dp", None)),
        out_specs=(token, token, token, P(("dp", "seq"), None)),
        check_vma=False,
    )
```

```python
import functools
import math

import jax
import jax.numpy as jnp
from jax import lax
from jax.experimental import pallas as pl
from jax.experimental.pallas import tpu as pltpu
from jax.sharding import PartitionSpec as P

HD = 128
MOST = 512
SUB = 128
NEG = -1e30


def attention_kernel(
    prior, group, q_ref, g_ref, k_ref, v_ref, sq_ref, sk_ref,
    dq_ref, dkp_ref, dvp_ref, dko_ref, dvo_ref, bias, dk, dv,
):
    local_len = q_ref.shape[0]
    window = k_ref.shape[0]
    span = MOST + SUB
    scale = HD ** (-0.5)
    exp_scale = scale * math.log2(math.e)

    @pl.when(pl.program_id(0) == 0)
    def _():
        key_pos = lax.broadcasted_iota(jnp.int32, (window, local_len), 0) - prior
        row_pos = lax.broadcasted_iota(jnp.int32, (window, local_len), 1)
        allowed = (sk_ref[...] == sq_ref[...]) & (key_pos <= row_pos)
        bias[...] = jnp.where(allowed, 0.0, NEG)

    dk[...] = jnp.zeros_like(dk)
    dv[...] = jnp.zeros_like(dv)
    nt = (((1,), (1,)), ((), ()))
    for r in range(local_len // SUB):
        rows = slice(r * SUB, (r + 1) * SUB)
        start = prior - MOST + r * SUB
        keys = slice(start, start + span)
        k = k_ref[keys, :]
        v = v_ref[keys, :]
        kt = k.T
        part_bias = bias[keys, rows]
        part_bias = jnp.concatenate([part_bias, part_bias], axis=1)
        for pair in range(group // 2):
            a = slice(2 * pair * HD, (2 * pair + 1) * HD)
            b = slice((2 * pair + 1) * HD, (2 * pair + 2) * HD)
            q = jnp.concatenate([q_ref[rows, a], q_ref[rows, b]], axis=0)
            g = jnp.concatenate([g_ref[rows, a], g_ref[rows, b]], axis=0)
            s = lax.dot_general(k, q, nt, preferred_element_type=jnp.float32)
            s = s * exp_scale + part_bias
            e = jnp.exp2(s - jnp.max(s, axis=0, keepdims=True))
            inv = 1.0 / jnp.sum(e, axis=0, keepdims=True)
            dp = lax.dot_general(v, g, nt, preferred_element_type=jnp.float32)
            p = e * inv
            delta = jnp.sum(p * dp, axis=0, keepdims=True)
            ds = (p * ((dp - delta) * scale)).astype(jnp.bfloat16)
            dv[keys, :] += jnp.dot(p.astype(jnp.bfloat16), g, preferred_element_type=jnp.float32)
            dk[keys, :] += jnp.dot(ds, q, preferred_element_type=jnp.float32)
            dqt = jnp.dot(kt, ds, preferred_element_type=jnp.float32)
            dq_ref[rows, a] = dqt[:, :SUB].T.astype(jnp.bfloat16)
            dq_ref[rows, b] = dqt[:, SUB:].T.astype(jnp.bfloat16)
    dkp_ref[...] = dk[:prior, :].astype(jnp.bfloat16)
    dvp_ref[...] = dv[:prior, :].astype(jnp.bfloat16)
    dko_ref[...] = dk[prior:, :]
    dvo_ref[...] = dv[prior:, :]


def attention_grads(q, g, window_kv, seg_rows, seg_keys):
    local_len, width = q.shape
    window = window_kv.shape[0]
    kv_width = window_kv.shape[1] // 2
    kv_heads = kv_width // HD
    group = width // HD // kv_heads
    prior = window - local_len
    wide = lambda n, w: pl.BlockSpec((n, w), lambda i: (0, i))
    whole = lambda s: pl.BlockSpec(s, lambda i: (0, 0))
    elements = window * local_len * kv_heads * group
    return pl.pallas_call(
        functools.partial(attention_kernel, prior, group),
        grid=(kv_heads,),
        in_specs=[
            wide(local_len, group * HD),
            wide(local_len, group * HD),
            wide(window, HD),
            pl.BlockSpec((window, HD), lambda i: (0, i + kv_heads)),
            whole((1, local_len)),
            whole((window, 1)),
        ],
        out_specs=[
            wide(local_len, group * HD),
            wide(prior, HD),
            wide(prior, HD),
            wide(local_len, HD),
            wide(local_len, HD),
        ],
        out_shape=[
            jax.ShapeDtypeStruct((local_len, width), jnp.bfloat16),
            jax.ShapeDtypeStruct((prior, kv_width), jnp.bfloat16),
            jax.ShapeDtypeStruct((prior, kv_width), jnp.bfloat16),
            jax.ShapeDtypeStruct((local_len, kv_width), jnp.float32),
            jax.ShapeDtypeStruct((local_len, kv_width), jnp.float32),
        ],
        scratch_shapes=[
            pltpu.VMEM((window, local_len), jnp.float32),
            pltpu.VMEM((window, HD), jnp.float32),
            pltpu.VMEM((window, HD), jnp.float32),
        ],
        compiler_params=pltpu.CompilerParams(vmem_limit_bytes=40 * 1024 * 1024),
        cost_estimate=pl.CostEstimate(
            flops=10 * elements * HD, bytes_accessed=10 * 1024 * 1024, transcendentals=elements
        ),
    )(q, g, window_kv, window_kv, seg_rows, seg_keys)


def shards(queries, key_states, value_states, out_grad, layer_input, lengths):
    seq_count = lax.axis_size("seq")
    dp_count = lax.axis_size("dp")
    me = lax.axis_index("seq")
    streams, local_len, query_width = queries.shape
    kv_width = key_states.shape[2]
    width = layer_input.shape[2]
    full_len = local_len * seq_count
    steps = -(-MOST // local_len)
    prior = steps * local_len
    piece = width // (dp_count * seq_count)

    own_kv = jnp.concatenate([key_states, value_states], axis=2)
    shifted = [
        lax.ppermute(own_kv, "seq", [(i, i + s) for i in range(seq_count - s)])
        if s < seq_count else jnp.zeros_like(own_kv)
        for s in range(steps, 0, -1)
    ]

    both = ("dp", "seq")
    pair = 2 if dp_count % 2 == 0 else 1
    members = pair * seq_count
    groups = dp_count // pair
    member = lax.rem(lax.axis_index("dp"), pair) * seq_count + me
    split_input = layer_input.reshape(streams * local_len, groups, members, piece)

    def columns_of(owner):
        block = lax.dynamic_slice_in_dim(split_input, owner, 1, axis=2)
        return block.reshape(streams * local_len, groups * piece)

    def ring(s):
        return [
            (z * members + i, z * members + (i + s) % members)
            for z in range(groups) for i in range(members)
        ]

    inputs = [columns_of(member)] + [
        lax.ppermute(columns_of(lax.rem(member + s, members)), both, ring(s))
        for s in range(1, members)
    ]
    all_inputs = jnp.concatenate(inputs, axis=0)

    positions = jnp.arange(full_len, dtype=jnp.int32)
    samples = jnp.arange(lengths.shape[1], dtype=jnp.int32)
    ends = jnp.sum(jnp.where(samples[None, :] <= samples[:, None], lengths[:, None, :], 0), axis=2)
    segments = jnp.sum((ends[:, None, :] <= positions[None, :, None]).astype(jnp.int32), axis=2)
    padded = jnp.concatenate([jnp.full((streams, prior), -1, jnp.int32), segments], axis=1)
    seg_window = lax.dynamic_slice_in_dim(padded, me * local_len, prior + local_len, axis=1)

    window_kv = jnp.concatenate(shifted + [own_kv], axis=1)
    results = [
        attention_grads(
            queries[i], out_grad[i], window_kv[i],
            seg_window[i, prior:].reshape(1, local_len), seg_window[i].reshape(-1, 1),
        )
        for i in range(streams)
    ]
    query_grad, key_prior, value_prior, key_own, value_own = (jnp.stack(x) for x in zip(*results))

    def collect(own, parts):
        total = own
        for n, s in enumerate(range(steps, 0, -1)):
            if s < seq_count:
                block = parts[:, n * local_len:(n + 1) * local_len]
                total = total + lax.ppermute(
                    block, "seq", [(i + s, i) for i in range(seq_count - s)]
                ).astype(jnp.float32)
        return total.astype(jnp.bfloat16)

    value_grad = collect(value_own, value_prior)
    key_grad = collect(key_own, key_prior)

    flat_value = value_grad.reshape(streams * local_len, kv_width)
    all_values = jnp.concatenate(
        [flat_value] + [lax.ppermute(flat_value, both, ring(s)) for s in range(1, members)],
        axis=0,
    )
    partial = lax.dot_general(
        all_inputs, all_values, (((0,), (0,)), ((), ())), preferred_element_type=jnp.float32
    ) / math.sqrt(streams * dp_count * full_len)
    mine = lax.axis_index("dp") // pair
    partial = partial.reshape(groups, piece, kv_width)
    weight_grad = lax.dynamic_index_in_dim(partial, mine, 0, keepdims=False)
    halved = partial.astype(jnp.bfloat16)
    for s in range(1, groups):
        block = lax.dynamic_index_in_dim(halved, lax.rem(mine + s, groups), 0, keepdims=False)
        turn = [(i, (i + s * pair) % dp_count) for i in range(dp_count)]
        weight_grad = weight_grad + lax.ppermute(block, "dp", turn).astype(jnp.float32)
    return (query_grad, key_grad, value_grad, weight_grad)


def solution(mesh):
    token = P("dp", "seq", None)
    return jax.shard_map(
        shards,
        mesh=mesh,
        in_specs=(token, token, token, token, token, P("dp", None)),
        out_specs=(token, token, token, P(("dp", "seq"), None)),
        check_vma=False,
    )
```

```python
import functools
import math

import jax
import jax.numpy as jnp
from jax import lax
from jax.experimental import pallas as pl
from jax.experimental.pallas import tpu as pltpu
from jax.sharding import PartitionSpec as P

HD = 128
MOST = 512
SUB = 128
NEG = -1e30


def attention_kernel(
    prior, group, q_ref, g_ref, k_ref, v_ref, sq_ref, sk_ref,
    dq_ref, dkp_ref, dvp_ref, dko_ref, dvo_ref, bias, dk, dv,
):
    local_len = q_ref.shape[0]
    window = k_ref.shape[0]
    span = MOST + SUB
    scale = HD ** (-0.5)
    exp_scale = scale * math.log2(math.e)

    @pl.when(pl.program_id(0) == 0)
    def _():
        key_pos = lax.broadcasted_iota(jnp.int32, (window, local_len), 0) - prior
        row_pos = lax.broadcasted_iota(jnp.int32, (window, local_len), 1)
        allowed = (sk_ref[...] == sq_ref[...]) & (key_pos <= row_pos)
        bias[...] = jnp.where(allowed, 0.0, NEG)

    dk[...] = jnp.zeros_like(dk)
    dv[...] = jnp.zeros_like(dv)
    nt = (((1,), (1,)), ((), ()))
    for r in range(local_len // SUB):
        rows = slice(r * SUB, (r + 1) * SUB)
        start = prior - MOST + r * SUB
        keys = slice(start, start + span)
        k = k_ref[keys, :]
        v = v_ref[keys, :]
        kt = k.T
        part_bias = bias[keys, rows]
        part_bias = jnp.concatenate([part_bias, part_bias], axis=1)
        for pair in range(group // 2):
            a = slice(2 * pair * HD, (2 * pair + 1) * HD)
            b = slice((2 * pair + 1) * HD, (2 * pair + 2) * HD)
            q = jnp.concatenate([q_ref[rows, a], q_ref[rows, b]], axis=0)
            g = jnp.concatenate([g_ref[rows, a], g_ref[rows, b]], axis=0)
            s = lax.dot_general(k, q, nt, preferred_element_type=jnp.float32)
            s = s * exp_scale + part_bias
            e = jnp.exp2(s - jnp.max(s, axis=0, keepdims=True))
            inv = 1.0 / jnp.sum(e, axis=0, keepdims=True)
            dp = lax.dot_general(v, g, nt, preferred_element_type=jnp.float32)
            p = e * inv
            delta = jnp.sum(p * dp, axis=0, keepdims=True)
            ds = (p * ((dp - delta) * scale)).astype(jnp.bfloat16)
            dv[keys, :] += jnp.dot(p.astype(jnp.bfloat16), g, preferred_element_type=jnp.float32)
            dk[keys, :] += jnp.dot(ds, q, preferred_element_type=jnp.float32)
            dqt = jnp.dot(kt, ds, preferred_element_type=jnp.float32)
            dq_ref[rows, a] = dqt[:, :SUB].T.astype(jnp.bfloat16)
            dq_ref[rows, b] = dqt[:, SUB:].T.astype(jnp.bfloat16)
    dkp_ref[...] = dk[:prior, :].astype(jnp.bfloat16)
    dvp_ref[...] = dv[:prior, :].astype(jnp.bfloat16)
    dko_ref[...] = dk[prior:, :]
    dvo_ref[...] = dv[prior:, :]


def attention_grads(q, g, window_kv, seg_rows, seg_keys):
    local_len, width = q.shape
    window = window_kv.shape[0]
    kv_width = window_kv.shape[1] // 2
    kv_heads = kv_width // HD
    group = width // HD // kv_heads
    prior = window - local_len
    wide = lambda n, w: pl.BlockSpec((n, w), lambda i: (0, i))
    whole = lambda s: pl.BlockSpec(s, lambda i: (0, 0))
    elements = window * local_len * kv_heads * group
    return pl.pallas_call(
        functools.partial(attention_kernel, prior, group),
        grid=(kv_heads,),
        in_specs=[
            wide(local_len, group * HD),
            wide(local_len, group * HD),
            wide(window, HD),
            pl.BlockSpec((window, HD), lambda i: (0, i + kv_heads)),
            whole((1, local_len)),
            whole((window, 1)),
        ],
        out_specs=[
            wide(local_len, group * HD),
            wide(prior, HD),
            wide(prior, HD),
            wide(local_len, HD),
            wide(local_len, HD),
        ],
        out_shape=[
            jax.ShapeDtypeStruct((local_len, width), jnp.bfloat16),
            jax.ShapeDtypeStruct((prior, kv_width), jnp.bfloat16),
            jax.ShapeDtypeStruct((prior, kv_width), jnp.bfloat16),
            jax.ShapeDtypeStruct((local_len, kv_width), jnp.float32),
            jax.ShapeDtypeStruct((local_len, kv_width), jnp.float32),
        ],
        scratch_shapes=[
            pltpu.VMEM((window, local_len), jnp.float32),
            pltpu.VMEM((window, HD), jnp.float32),
            pltpu.VMEM((window, HD), jnp.float32),
        ],
        compiler_params=pltpu.CompilerParams(vmem_limit_bytes=40 * 1024 * 1024),
        cost_estimate=pl.CostEstimate(
            flops=10 * elements * HD, bytes_accessed=10 * 1024 * 1024, transcendentals=elements
        ),
    )(q, g, window_kv, window_kv, seg_rows, seg_keys)


def shards(queries, key_states, value_states, out_grad, layer_input, lengths):
    seq_count = lax.axis_size("seq")
    dp_count = lax.axis_size("dp")
    me = lax.axis_index("seq")
    streams, local_len, query_width = queries.shape
    kv_width = key_states.shape[2]
    width = layer_input.shape[2]
    full_len = local_len * seq_count
    steps = -(-MOST // local_len)
    prior = steps * local_len
    piece = width // (dp_count * seq_count)

    own_kv = jnp.concatenate([key_states, value_states], axis=2)
    shifted = [
        lax.ppermute(own_kv, "seq", [(i, i + s) for i in range(seq_count - s)])
        if s < seq_count else jnp.zeros_like(own_kv)
        for s in range(steps, 0, -1)
    ]

    both = ("dp", "seq")
    pair = 2 if dp_count % 2 == 0 else 1
    members = pair * seq_count
    groups = dp_count // pair
    member = lax.rem(lax.axis_index("dp"), pair) * seq_count + me
    split_input = layer_input.reshape(streams * local_len, groups, members, piece)

    def columns_of(owner):
        block = lax.dynamic_slice_in_dim(split_input, owner, 1, axis=2)
        return block.reshape(streams * local_len, groups * piece)

    def flip(t):
        return [
            (z * members + i, z * members + (i ^ t)) for z in range(groups) for i in range(members)
        ]

    order, bit = [0], members // 2
    while bit:
        order = order + [t ^ bit for t in order]
        bit //= 2
    inputs = [columns_of(member)] + [
        lax.ppermute(columns_of(jnp.bitwise_xor(member, t)), both, flip(t)) for t in order[1:]
    ]
    all_inputs = jnp.concatenate(inputs, axis=0)

    positions = jnp.arange(full_len, dtype=jnp.int32)
    samples = jnp.arange(lengths.shape[1], dtype=jnp.int32)
    ends = jnp.sum(jnp.where(samples[None, :] <= samples[:, None], lengths[:, None, :], 0), axis=2)
    segments = jnp.sum((ends[:, None, :] <= positions[None, :, None]).astype(jnp.int32), axis=2)
    padded = jnp.concatenate([jnp.full((streams, prior), -1, jnp.int32), segments], axis=1)
    seg_window = lax.dynamic_slice_in_dim(padded, me * local_len, prior + local_len, axis=1)

    window_kv = jnp.concatenate(shifted + [own_kv], axis=1)
    results = [
        attention_grads(
            queries[i], out_grad[i], window_kv[i],
            seg_window[i, prior:].reshape(1, local_len), seg_window[i].reshape(-1, 1),
        )
        for i in range(streams)
    ]
    query_grad, key_prior, value_prior, key_own, value_own = (jnp.stack(x) for x in zip(*results))

    def collect(own, parts):
        total = own
        for n, s in enumerate(range(steps, 0, -1)):
            if s < seq_count:
                block = parts[:, n * local_len:(n + 1) * local_len]
                total = total + lax.ppermute(
                    block, "seq", [(i + s, i) for i in range(seq_count - s)]
                ).astype(jnp.float32)
        return total.astype(jnp.bfloat16)

    value_grad = collect(value_own, value_prior)
    key_grad = collect(key_own, key_prior)

    flat_value = value_grad.reshape(streams * local_len, kv_width)
    all_values, bit = flat_value, members // 2
    while bit:
        received = lax.ppermute(all_values, both, flip(bit))
        all_values = jnp.concatenate([all_values, received], axis=0)
        bit //= 2
    partial = lax.dot_general(
        all_inputs, all_values, (((0,), (0,)), ((), ())), preferred_element_type=jnp.float32
    ) / math.sqrt(streams * dp_count * full_len)
    mine = lax.axis_index("dp") // pair
    partial = partial.reshape(groups, piece, kv_width)
    weight_grad = lax.dynamic_index_in_dim(partial, mine, 0, keepdims=False)
    halved = partial.astype(jnp.bfloat16)
    for s in range(1, groups):
        block = lax.dynamic_index_in_dim(halved, lax.rem(mine + s, groups), 0, keepdims=False)
        turn = [(i, (i + s * pair) % dp_count) for i in range(dp_count)]
        weight_grad = weight_grad + lax.ppermute(block, "dp", turn).astype(jnp.float32)
    return (query_grad, key_grad, value_grad, weight_grad)


def solution(mesh):
    token = P("dp", "seq", None)
    return jax.shard_map(
        shards,
        mesh=mesh,
        in_specs=(token, token, token, token, token, P("dp", None)),
        out_specs=(token, token, token, P(("dp", "seq"), None)),
        check_vma=False,
    )
```

```python
import functools
import math

import jax
import jax.numpy as jnp
from jax import lax
from jax.experimental import pallas as pl
from jax.experimental.pallas import tpu as pltpu
from jax.sharding import PartitionSpec as P

HD = 128
MOST = 512
SUB = 128
NEG = -1e30


def attention_kernel(
    prior, group, q_ref, g_ref, k_ref, v_ref, sq_ref, sk_ref,
    dq_ref, dkp_ref, dvp_ref, dko_ref, dvo_ref, bias, dk, dv,
):
    local_len = q_ref.shape[0]
    window = k_ref.shape[0]
    span = MOST + SUB
    scale = HD ** (-0.5)
    exp_scale = scale * math.log2(math.e)

    @pl.when(pl.program_id(0) == 0)
    def _():
        key_pos = lax.broadcasted_iota(jnp.int32, (window, local_len), 0) - prior
        row_pos = lax.broadcasted_iota(jnp.int32, (window, local_len), 1)
        allowed = (sk_ref[...] == sq_ref[...]) & (key_pos <= row_pos)
        bias[...] = jnp.where(allowed, 0.0, NEG)

    dk[...] = jnp.zeros_like(dk)
    dv[...] = jnp.zeros_like(dv)
    nt = (((1,), (1,)), ((), ()))
    for r in range(local_len // SUB):
        rows = slice(r * SUB, (r + 1) * SUB)
        start = prior - MOST + r * SUB
        keys = slice(start, start + span)
        k = k_ref[keys, :]
        v = v_ref[keys, :]
        kt = k.T
        part_bias = bias[keys, rows]
        part_bias = jnp.concatenate([part_bias, part_bias], axis=1)
        for pair in range(group // 2):
            a = slice(2 * pair * HD, (2 * pair + 1) * HD)
            b = slice((2 * pair + 1) * HD, (2 * pair + 2) * HD)
            q = jnp.concatenate([q_ref[rows, a], q_ref[rows, b]], axis=0)
            g = jnp.concatenate([g_ref[rows, a], g_ref[rows, b]], axis=0)
            s = lax.dot_general(k, q, nt, preferred_element_type=jnp.float32)
            s = s * exp_scale + part_bias
            e = jnp.exp2(s - jnp.max(s, axis=0, keepdims=True))
            inv = 1.0 / jnp.sum(e, axis=0, keepdims=True)
            dp = lax.dot_general(v, g, nt, preferred_element_type=jnp.float32)
            p = e * inv
            delta = jnp.sum(p * dp, axis=0, keepdims=True)
            ds = (p * ((dp - delta) * scale)).astype(jnp.bfloat16)
            dv[keys, :] += jnp.dot(p.astype(jnp.bfloat16), g, preferred_element_type=jnp.float32)
            dk[keys, :] += jnp.dot(ds, q, preferred_element_type=jnp.float32)
            dqt = jnp.dot(kt, ds, preferred_element_type=jnp.float32)
            dq_ref[rows, a] = dqt[:, :SUB].T.astype(jnp.bfloat16)
            dq_ref[rows, b] = dqt[:, SUB:].T.astype(jnp.bfloat16)
    dkp_ref[...] = dk[:prior, :].astype(jnp.bfloat16)
    dvp_ref[...] = dv[:prior, :].astype(jnp.bfloat16)
    dko_ref[...] = dk[prior:, :]
    dvo_ref[...] = dv[prior:, :]


def attention_grads(q, g, window_kv, seg_rows, seg_keys):
    local_len, width = q.shape
    window = window_kv.shape[0]
    kv_width = window_kv.shape[1] // 2
    kv_heads = kv_width // HD
    group = width // HD // kv_heads
    prior = window - local_len
    wide = lambda n, w: pl.BlockSpec((n, w), lambda i: (0, i))
    whole = lambda s: pl.BlockSpec(s, lambda i: (0, 0))
    elements = window * local_len * kv_heads * group
    return pl.pallas_call(
        functools.partial(attention_kernel, prior, group),
        grid=(kv_heads,),
        in_specs=[
            wide(local_len, group * HD),
            wide(local_len, group * HD),
            wide(window, HD),
            pl.BlockSpec((window, HD), lambda i: (0, i + kv_heads)),
            whole((1, local_len)),
            whole((window, 1)),
        ],
        out_specs=[
            wide(local_len, group * HD),
            wide(prior, HD),
            wide(prior, HD),
            wide(local_len, HD),
            wide(local_len, HD),
        ],
        out_shape=[
            jax.ShapeDtypeStruct((local_len, width), jnp.bfloat16),
            jax.ShapeDtypeStruct((prior, kv_width), jnp.bfloat16),
            jax.ShapeDtypeStruct((prior, kv_width), jnp.bfloat16),
            jax.ShapeDtypeStruct((local_len, kv_width), jnp.float32),
            jax.ShapeDtypeStruct((local_len, kv_width), jnp.float32),
        ],
        scratch_shapes=[
            pltpu.VMEM((window, local_len), jnp.float32),
            pltpu.VMEM((window, HD), jnp.float32),
            pltpu.VMEM((window, HD), jnp.float32),
        ],
        compiler_params=pltpu.CompilerParams(vmem_limit_bytes=40 * 1024 * 1024),
        cost_estimate=pl.CostEstimate(
            flops=10 * elements * HD, bytes_accessed=10 * 1024 * 1024, transcendentals=elements
        ),
    )(q, g, window_kv, window_kv, seg_rows, seg_keys)


def shards(queries, key_states, value_states, out_grad, layer_input, lengths):
    seq_count = lax.axis_size("seq")
    dp_count = lax.axis_size("dp")
    me = lax.axis_index("seq")
    streams, local_len, query_width = queries.shape
    kv_width = key_states.shape[2]
    width = layer_input.shape[2]
    full_len = local_len * seq_count
    steps = -(-MOST // local_len)
    prior = steps * local_len
    piece = width // (dp_count * seq_count)

    own_kv = jnp.concatenate([key_states, value_states], axis=2)
    shifted = [
        lax.ppermute(own_kv, "seq", [(i, i + s) for i in range(seq_count - s)])
        if s < seq_count else jnp.zeros_like(own_kv)
        for s in range(steps, 0, -1)
    ]

    both = ("dp", "seq")
    pair = 2 if dp_count % 2 == 0 else 1
    members = pair * seq_count
    groups = dp_count // pair
    member = lax.rem(lax.axis_index("dp"), pair) * seq_count + me
    split_input = layer_input.reshape(streams * local_len, groups, members, piece)

    def columns_of(owner):
        block = lax.dynamic_slice_in_dim(split_input, owner, 1, axis=2)
        return block.reshape(streams * local_len, groups * piece)

    def flip(t):
        return [
            (z * members + i, z * members + (i ^ t)) for z in range(groups) for i in range(members)
        ]

    order, bit = [0], members // 2
    while bit:
        order = order + [t ^ bit for t in order]
        bit //= 2
    inputs = [columns_of(member)] + [
        lax.ppermute(columns_of(jnp.bitwise_xor(member, t)), both, flip(t)) for t in order[1:]
    ]
    positions = jnp.arange(full_len, dtype=jnp.int32)
    samples = jnp.arange(lengths.shape[1], dtype=jnp.int32)
    ends = jnp.sum(jnp.where(samples[None, :] <= samples[:, None], lengths[:, None, :], 0), axis=2)
    segments = jnp.sum((ends[:, None, :] <= positions[None, :, None]).astype(jnp.int32), axis=2)
    padded = jnp.concatenate([jnp.full((streams, prior), -1, jnp.int32), segments], axis=1)
    seg_window = lax.dynamic_slice_in_dim(padded, me * local_len, prior + local_len, axis=1)

    window_kv = jnp.concatenate(shifted + [own_kv], axis=1)
    results = [
        attention_grads(
            queries[i], out_grad[i], window_kv[i],
            seg_window[i, prior:].reshape(1, local_len), seg_window[i].reshape(-1, 1),
        )
        for i in range(streams)
    ]
    query_grad, key_prior, value_prior, key_own, value_own = (jnp.stack(x) for x in zip(*results))

    def collect(own, parts):
        total = own
        for n, s in enumerate(range(steps, 0, -1)):
            if s < seq_count:
                block = parts[:, n * local_len:(n + 1) * local_len]
                total = total + lax.ppermute(
                    block, "seq", [(i + s, i) for i in range(seq_count - s)]
                ).astype(jnp.float32)
        return total.astype(jnp.bfloat16)

    value_prior, *inputs = lax.optimization_barrier((value_prior, *inputs))
    all_inputs = jnp.concatenate(inputs, axis=0)
    value_grad = collect(value_own, value_prior)
    key_grad = collect(key_own, key_prior)

    flat_value = value_grad.reshape(streams * local_len, kv_width)
    all_values, bit = flat_value, members // 2
    while bit:
        received = lax.ppermute(all_values, both, flip(bit))
        all_values = jnp.concatenate([all_values, received], axis=0)
        bit //= 2
    partial = lax.dot_general(
        all_inputs, all_values, (((0,), (0,)), ((), ())), preferred_element_type=jnp.float32
    ) / math.sqrt(streams * dp_count * full_len)
    mine = lax.axis_index("dp") // pair
    partial = partial.reshape(groups, piece, kv_width)
    weight_grad = lax.dynamic_index_in_dim(partial, mine, 0, keepdims=False)
    halved = partial.astype(jnp.bfloat16)
    for s in range(1, groups):
        block = lax.dynamic_index_in_dim(halved, lax.rem(mine + s, groups), 0, keepdims=False)
        turn = [(i, (i + s * pair) % dp_count) for i in range(dp_count)]
        weight_grad = weight_grad + lax.ppermute(block, "dp", turn).astype(jnp.float32)
    return (query_grad, key_grad, value_grad, weight_grad)


def solution(mesh):
    token = P("dp", "seq", None)
    return jax.shard_map(
        shards,
        mesh=mesh,
        in_specs=(token, token, token, token, token, P("dp", None)),
        out_specs=(token, token, token, P(("dp", "seq"), None)),
        check_vma=False,
    )
```
